32 devices in a mesh: dp: 8 (over y, x, core), cent: 4 (over z).
Axes of the slice: x: 2, y: 2, z: 4, core: 2. Of those that a mesh axis runs over, the one named last changes fastest.
Arguments:
- embeddings: bfloat16 [8192, 768], P(('dp', 'cent')), may hold values from -6 to 6
- centroids: bfloat16 [2048, 768], P('cent'), may hold values from -6 to 6
- assign: int32 [8192], P(('dp', 'cent')), may hold values from 0 to 2047, as said below
- bins: int32 [8192], P(('dp', 'cent')), may hold values from 0 to 255
Outputs:
- quant_error: float32 [8192], P(('dp', 'cent'))
- new_centroids: float32 [2048, 768], P(('cent', 'dp'))
- histograms: float32 [2048, 256], P(('cent', 'dp'))
The draws below stay inside these ranges and needn't reach their ends.
Inputs may be any that keep to these rules, and one draw needn't show every extreme that they name: `assign`: list k belongs to owner k // 64; among the 256 rows of one device (aligned blocks) at most 16 name lists of any one owner.
All inputs are finite; a program needn't handle non-finite values.
Results may differ from the reference program's by a relative error of at most 0.0003.
Values may be sent and summed in bfloat16 or wider, within the bound.
A program may use at most 128 MiB of HBM per device.

```python
import jax
import jax.numpy as jnp
from jax import lax

D = 768
LISTS_DEV = 64
NBINS = 256
ROWS_DEV = 256
K = 2048
ROWS = 8192
CAP = 16
DEVICES = 32


def draw_assign(key, part):
    owner_total = DEVICES
    slot_cap = CAP
    hot_total = max(1, DEVICES // 16)
    slot_total = owner_total * slot_cap
    score_top = max(2, 2 ** 29 // slot_total)
    key_hot, key_blocks, key_local = jax.random.split(key, 3)
    hot_perm = jax.random.permutation(key_hot, owner_total)
    hot_flag = jnp.zeros((owner_total,), jnp.int32).at[hot_perm[:hot_total]].set(1)
    slot_ids = jnp.arange(slot_total, dtype=jnp.int32)
    owner_of = slot_ids // slot_cap

    def one_block(block_key):
        key_score, key_shuffle = jax.random.split(block_key)
        scores = jax.random.randint(key_score, (slot_total,), 0, score_top)
        ranked_key = scores * slot_total + slot_ids + hot_flag[owner_of] * 2 ** 30
        ranked = jnp.argsort(-ranked_key)
        chosen = owner_of[ranked[:ROWS_DEV]]
        shuffle = jax.random.permutation(key_shuffle, ROWS_DEV)
        return chosen[shuffle]
    owners = jax.vmap(one_block)(jax.random.split(key_blocks, DEVICES))
    local_list = jax.random.randint(key_local, (DEVICES, ROWS_DEV), 0, LISTS_DEV)
    return (owners * LISTS_DEV + local_list).reshape(ROWS).astype(jnp.int32)


def with_ends(result, rng, smallest, largest):
    place = [jax.random.randint(jax.random.fold_in(rng, axis), (), 0, length) for axis, length in enumerate(result.shape)]
    widest = result.shape.index(max(result.shape))
    beside = place[:widest] + [(place[widest] + 1) % result.shape[widest]] + place[widest + 1:]
    return result.at[tuple(place)].set(smallest).at[tuple(beside)].set(largest)


def block_scale(stream_key, shape, cuts, smallest, top_value):
    factor_of, own = 1.0, jax.random.fold_in(stream_key, 6)
    for position, shards_of in cuts:
        draws = jnp.exp(jax.random.uniform(jax.random.fold_in(own, position), (shards_of,), jnp.float32, smallest / len(cuts), top_value / len(cuts)))
        factor_of = factor_of * jnp.repeat(draws, shape[position] // shards_of).reshape([-1 if axis == position else 1 for axis in range(len(shape))])
    return factor_of


def bell_draw(stream_key, shape, scale, most, cuts=(), kind=jnp.bfloat16):
    result = jax.random.normal(stream_key, shape, jnp.float32) * scale
    if len(cuts) > 0:
        result = block_scale(stream_key, shape, cuts, -0.22, 0.18) * result
    return jnp.clip(result, min=-most, max=most).astype(kind)


def setup_inputs(seed: int = 0) -> dict:
    key_list = jax.random.split(jax.random.key(seed), 5)
    embeddings = bell_draw(key_list[0], (ROWS, D), 1.0, 6.0, ((0, 32),))
    centroids = bell_draw(key_list[1], (K, D), 1.0, 6.0, ((0, 4),))
    assign = draw_assign(jax.random.fold_in(key_list[4], 71), 0)
    bins = with_ends(jax.random.randint(key_list[3], (ROWS,), 0, NBINS), jax.random.fold_in(key_list[3], 1), 0, NBINS - 1).astype(jnp.int32)
    return dict(embeddings=embeddings, centroids=centroids, assign=assign, bins=bins)


epsilon = 1e-06

def reference(embeddings, centroids, assign, bins):
    cent_f32 = centroids.astype(jnp.float32)
    cent_sq = lax.optimization_barrier(jnp.sum(cent_f32 * cent_f32, axis=1))
    block_len = min(ROWS, 2048)
    row_blocks = embeddings.reshape(ROWS // block_len, block_len, D)

    def block_min(block_rows):
        products = jnp.dot(block_rows, centroids.T, preferred_element_type=jnp.float32)
        row_f32 = block_rows.astype(jnp.float32)
        row_sq = lax.optimization_barrier(jnp.sum(row_f32 * row_f32, axis=1))
        return lax.optimization_barrier(jnp.min(cent_sq[None, :] - 2.0 * products, axis=1)) + row_sq
    quant_error = lax.map(block_min, row_blocks).reshape(ROWS) / D
    residual = embeddings.astype(jnp.float32) - cent_f32[assign]
    residual_sums = jax.ops.segment_sum(residual, assign, num_segments=K)
    counts = jax.ops.segment_sum(jnp.ones((ROWS,), jnp.float32), assign, num_segments=K)
    new_centroids = cent_f32 + residual_sums / jnp.maximum(counts, 1.0)[:, None]
    residual_norm = jnp.sqrt(lax.optimization_barrier(jnp.mean(residual * residual, axis=1)) + epsilon)
    histograms = jnp.zeros((K, NBINS), jnp.float32).at[assign, bins].add(residual_norm)
    return (quant_error, new_centroids, histograms)
```

```python
import functools

import jax
import jax.numpy as jnp
from jax import lax
from jax.experimental import pallas as pl
from jax.experimental.pallas import tpu as pltpu
from jax.sharding import PartitionSpec as P

LISTS_DEV = 64
NBINS = 256
TAGS = 128

epsilon = 1e-06
MESH = pl.DeviceIdType.MESH
NT = (((1,), (1,)), ((), ()))


def kernel(
    n_dp, n_cent, cap,
    emb_ref, cent_ref, assign_ref, bins_ref,
    quant_ref, new_ref, hist_ref,
    outbuf, inbuf, mate_rows, pieces, min_out, min_in,
    row_send, row_recv, mate_send, mate_recv, z_send, z_recv, p_send, p_recv, m_send, m_recv,
):
    rows, dim = emb_ref.shape
    lists = cent_ref.shape[0] // n_dp
    chips = n_dp // 2
    owners = n_dp * n_cent
    slots = owners * cap
    dp, ce = lax.axis_index("dp"), lax.axis_index("cent")
    chip, core = dp // 2, dp % 2
    mate = chip * 2 + (1 - core)
    me = ce * n_dp + dp

    barrier = pltpu.get_barrier_semaphore()

    def greet(i, _):
        other = lax.rem(me + i, owners)
        pl.semaphore_signal(barrier, inc=1, device_id=(other % n_dp, other // n_dp), device_id_type=MESH)
        return 0

    lax.fori_loop(1, owners, greet, 0)

    shift = lists.bit_length() - 1
    assign = assign_ref[...]
    owner = lax.shift_right_logical(assign, shift)
    local = assign - lax.shift_left(owner, shift)
    hits = lax.broadcasted_iota(jnp.int32, (owners, rows), 0) == owner
    hits_f = hits.astype(jnp.float32)
    before = lax.broadcasted_iota(jnp.int32, (rows, rows), 0) < lax.broadcasted_iota(jnp.int32, (rows, rows), 1)
    earlier = jnp.dot(
        hits_f.astype(jnp.bfloat16),
        before.astype(jnp.float32).astype(jnp.bfloat16),
        preferred_element_type=jnp.float32,
    )
    place = jnp.sum(earlier * hits_f, axis=0, keepdims=True)
    position = owner * cap + place.astype(jnp.int32)
    pick = (lax.broadcasted_iota(jnp.int32, (slots, rows), 0) == position).astype(jnp.float32).astype(jnp.bfloat16)
    tag_row = lax.broadcasted_iota(jnp.int32, (TAGS, rows), 0)
    tags = jnp.where(
        tag_row == 0,
        jnp.broadcast_to(local + 1, (TAGS, rows)),
        jnp.where(tag_row == 1, jnp.broadcast_to(bins_ref[...], (TAGS, rows)), 0),
    ).astype(jnp.float32).astype(jnp.bfloat16)
    outbuf[:, :, :dim] = (
        jnp.dot(pick, emb_ref[...], preferred_element_type=jnp.float32)
        .astype(jnp.bfloat16).reshape(owners, cap, dim)
    )
    outbuf[:, :, dim:] = (
        lax.dot_general(pick, tags, NT, preferred_element_type=jnp.float32)
        .astype(jnp.bfloat16).reshape(owners, cap, TAGS)
    )

    pl.semaphore_wait(barrier, owners - 1)

    def z_copy(i):
        other = lax.rem(ce + i, n_cent)
        return pltpu.make_async_remote_copy(
            src_ref=cent_ref.at[pl.ds(pl.multiple_of(dp * lists, lists), lists)],
            dst_ref=pieces.at[chip, ce],
            send_sem=z_send.at[other],
            recv_sem=z_recv.at[ce],
            device_id=(dp, other),
            device_id_type=MESH,
        )

    for i in range(1, n_cent):
        z_copy(i).start()
    mate_copy = pltpu.make_async_remote_copy(
        src_ref=emb_ref, dst_ref=mate_rows, send_sem=mate_send, recv_sem=mate_recv,
        device_id=(mate, ce), device_id_type=MESH,
    )
    mate_copy.start()

    def row_copy(other):
        return pltpu.make_async_remote_copy(
            src_ref=outbuf.at[other],
            dst_ref=inbuf.at[me],
            send_sem=row_send.at[other],
            recv_sem=row_recv.at[me],
            device_id=(other % n_dp, other // n_dp),
            device_id_type=MESH,
        )

    def send_rows(i, _):
        gap = i // n_dp + 1
        other = lax.rem(ce + gap, n_cent) * n_dp + lax.rem(dp + i, n_dp)
        row_copy(other).start()
        return 0

    lax.fori_loop(0, owners - n_dp, send_rows, 0)

    def send_plane(i, _):
        row_copy(ce * n_dp + lax.rem(dp + i, n_dp)).start()
        return 0

    lax.fori_loop(1, n_dp, send_plane, 0)
    inbuf[me] = outbuf[me]

    mate_copy.wait_recv()

    def nearest(piece):
        piece_f = piece.astype(jnp.float32)
        sq = jnp.sum(piece_f * piece_f, axis=1, keepdims=True)
        own = lax.dot_general(piece, emb_ref[...], NT, preferred_element_type=jnp.float32)
        theirs = lax.dot_general(piece, mate_rows[...], NT, preferred_element_type=jnp.float32)
        return (
            jnp.min(sq - 2.0 * own, axis=0, keepdims=True),
            jnp.min(sq - 2.0 * theirs, axis=0, keepdims=True),
        )

    def merge(a, b):
        return jnp.minimum(a[0], b[0]), jnp.minimum(a[1], b[1])

    def own_block(j, best):
        at = pl.multiple_of((j * 2 + core) * lists, lists)
        return merge(best, nearest(cent_ref[pl.ds(at, lists), :]))

    far = jnp.full((1, rows), 3e38, jnp.float32)
    best = lax.fori_loop(0, chips, own_block, (far, far))

    def plane_copy(i, block):
        other = lax.rem(chip + i, chips)
        return pltpu.make_async_remote_copy(
            src_ref=pieces.at[chip, block],
            dst_ref=pieces.at[chip, block],
            send_sem=p_send.at[other, block],
            recv_sem=p_recv.at[chip, block],
            device_id=(other * 2 + core, ce),
            device_id_type=MESH,
        )

    def arrive(ref, sem):
        return pltpu.make_async_copy(ref, ref, sem)

    order = [1, n_cent - 1] + list(range(2, n_cent - 1))
    for gap in order:
        block = lax.rem(ce + gap, n_cent)
        arrive(pieces.at[chip, block], z_recv.at[block]).wait()
        for i in range(1, chips):
            plane_copy(i, block).start()
        best = merge(best, nearest(pieces[chip, block]))
    for gap in order:
        block = lax.rem(ce + gap, n_cent)

        def other_chips(i, best):
            j = lax.rem(chip + i, chips)
            arrive(pieces.at[j, block], p_recv.at[j, block]).wait()
            return merge(best, nearest(pieces[j, block]))

        best = lax.fori_loop(1, chips, other_chips, best)

    min_out[...] = jnp.broadcast_to(best[1], min_out.shape)
    min_copy = pltpu.make_async_remote_copy(
        src_ref=min_out, dst_ref=min_in, send_sem=m_send, recv_sem=m_recv,
        device_id=(mate, ce), device_id_type=MESH,
    )
    min_copy.start()
    emb_f = emb_ref[...].astype(jnp.float32)
    row_sq = jnp.sum(emb_f * emb_f, axis=1, keepdims=True)
    row_sq = jnp.broadcast_to(row_sq, (rows, 128)).T[0:1]
    min_copy.wait()
    quant_ref[...] = (jnp.minimum(best[0], min_in[0:1]) + row_sq) * (1.0 / dim)

    def wait_rows(i, _):
        other = lax.rem(me + i, owners)
        arrive(inbuf.at[other], row_recv.at[other]).wait()
        return 0

    lax.fori_loop(1, owners, wait_rows, 0)
    own_rows = cent_ref[pl.ds(pl.multiple_of(dp * lists, lists), lists), :]
    arrived = inbuf[:, :, :dim].reshape(slots, dim)
    tags_in = inbuf[:, :, dim:].reshape(slots, TAGS).astype(jnp.float32)
    list_col = tags_in[:, 0:1].astype(jnp.int32) - 1
    bin_col = tags_in[:, 1:2].astype(jnp.int32)
    member = (lax.broadcasted_iota(jnp.int32, (slots, 128), 1) == list_col).astype(jnp.float32)
    member_t = member.T[:lists]
    member_b = member[:, :lists].astype(jnp.bfloat16)
    member_tb = member_t.astype(jnp.bfloat16)
    sums = jnp.dot(member_tb, arrived, preferred_element_type=jnp.float32)
    counts = jnp.sum(member_t, axis=1, keepdims=True)
    own_f = own_rows.astype(jnp.float32)
    new_ref[...] = own_f + (sums - counts * own_f) / jnp.maximum(counts, 1.0)
    residual = arrived.astype(jnp.float32) - jnp.dot(member_b, own_rows, preferred_element_type=jnp.float32)
    norm = jnp.sqrt(jnp.sum(residual * residual, axis=1, keepdims=True) * (1.0 / dim) + epsilon)
    in_bin = lax.broadcasted_iota(jnp.int32, (slots, NBINS), 1) == bin_col
    spread = jnp.where(in_bin, norm, 0.0)
    hist = jnp.zeros(hist_ref.shape, jnp.float32)
    for _ in range(3):
        part = spread.astype(jnp.bfloat16)
        hist = hist + jnp.dot(member_tb, part, preferred_element_type=jnp.float32)
        spread = spread - part.astype(jnp.float32)
    hist_ref[...] = hist

    mate_copy.wait_send()
    for i in range(1, n_cent):
        z_copy(i).wait_send()
    for gap in order:
        block = lax.rem(ce + gap, n_cent)
        for i in range(1, chips):
            plane_copy(i, block).wait_send()

    def sent(i, _):
        row_copy(lax.rem(me + i, owners)).wait_send()
        return 0

    lax.fori_loop(1, owners, sent, 0)


def per_device_kernel(embeddings, centroids, assign, bins):
    rows, dim = embeddings.shape
    n_dp, n_cent = lax.axis_size("dp"), lax.axis_size("cent")
    owners, chips = n_dp * n_cent, n_dp // 2
    cap = 2 * rows // owners
    lists = centroids.shape[0] // n_dp
    dma = pltpu.SemaphoreType.DMA
    vmem = pl.BlockSpec(memory_space=pltpu.VMEM)
    quant, new, hist = pl.pallas_call(
        functools.partial(kernel, n_dp, n_cent, cap),
        out_shape=(
            jax.ShapeDtypeStruct((1, rows), jnp.float32),
            jax.ShapeDtypeStruct((lists, dim), jnp.float32),
            jax.ShapeDtypeStruct((lists, NBINS), jnp.float32),
        ),
        in_specs=[vmem] * 4,
        out_specs=(vmem,) * 3,
        scratch_shapes=[
            pltpu.VMEM((owners, cap, dim + TAGS), jnp.bfloat16),
            pltpu.VMEM((owners, cap, dim + TAGS), jnp.bfloat16),
            pltpu.VMEM((rows, dim), jnp.bfloat16),
            pltpu.VMEM((chips, n_cent, lists, dim), jnp.bfloat16),
            pltpu.VMEM((8, rows), jnp.float32),
            pltpu.VMEM((8, rows), jnp.float32),
            dma((owners,)), dma((owners,)),
            dma, dma,
            dma((n_cent,)), dma((n_cent,)),
            dma((chips, n_cent)), dma((chips, n_cent)),
            dma, dma,
        ],
        compiler_params=pltpu.CompilerParams(
            collective_id=0, has_side_effects=True, vmem_limit_bytes=40 * 1024 * 1024
        ),
        cost_estimate=pl.CostEstimate(
            flops=2 * rows * 2048 * dim, bytes_accessed=4 * rows * dim * 2, transcendentals=0
        ),
    )(embeddings, centroids, assign.reshape(1, rows), bins.reshape(1, rows))
    return quant.reshape(rows), new, hist


def per_device_plain(embeddings, centroids, assign, bins):
    row_count, feature_dim = embeddings.shape
    row_f32 = embeddings.astype(jnp.float32)
    row_sq = jnp.sum(row_f32 * row_f32, axis=1)
    block_rows = lax.all_gather(centroids, "cent", axis=0, tiled=True)
    products = jnp.einsum("rd,kd->rk", embeddings, block_rows, preferred_element_type=jnp.float32)
    block_f32 = block_rows.astype(jnp.float32)
    cent_sq = jnp.sum(block_f32 * block_f32, axis=1)
    nearest_sq = jnp.min(cent_sq[None, :] - 2.0 * products, axis=1)
    quant_error = (nearest_sq + row_sq) / feature_dim
    dp_count = lax.axis_size("dp")
    cent_count = lax.axis_size("cent")
    owner_count = dp_count * cent_count
    slot_cap = 2 * row_count // owner_count
    owner_id = assign // LISTS_DEV
    local_list = assign % LISTS_DEV
    dest_slot = owner_id % dp_count * cent_count + owner_id // dp_count
    owner_hits = (dest_slot[:, None] == jnp.arange(owner_count, dtype=jnp.int32)[None, :]).astype(jnp.float32)
    row_ids = jnp.arange(row_count, dtype=jnp.int32)
    before = (row_ids[None, :] < row_ids[:, None]).astype(jnp.float32)
    earlier = jnp.dot(before, owner_hits)
    slot_id = jnp.sum(earlier * owner_hits, axis=1).astype(jnp.int32)
    position = dest_slot * slot_cap + slot_id
    outgoing = jnp.zeros((owner_count * slot_cap, feature_dim), jnp.bfloat16).at[position].set(embeddings)
    outgoing = outgoing.reshape(dp_count, cent_count, slot_cap, feature_dim)
    tag_values = jnp.stack([local_list, bins], axis=1).astype(jnp.float32)
    labels = jnp.full((owner_count * slot_cap, 2), -1.0, jnp.float32).at[position].set(tag_values)
    labels = labels.astype(jnp.bfloat16).reshape(dp_count, cent_count, slot_cap, 2)

    def exchange(x):
        x = lax.all_to_all(x, "dp", split_axis=0, concat_axis=0, tiled=True)
        return lax.all_to_all(x, "cent", split_axis=1, concat_axis=1, tiled=True)

    arrived = exchange(outgoing).reshape(-1, feature_dim).astype(jnp.float32)
    arrived_tags = exchange(labels).reshape(-1, 2).astype(jnp.int32)
    list_ids, bin_ids = arrived_tags[:, 0], arrived_tags[:, 1]
    member = (list_ids[:, None] == jnp.arange(LISTS_DEV, dtype=jnp.int32)[None, :]).astype(jnp.float32)
    own_rows = lax.dynamic_slice_in_dim(
        centroids, lax.axis_index("dp") * LISTS_DEV, LISTS_DEV, 0
    ).astype(jnp.float32)
    highest = lax.Precision.HIGHEST
    residual = arrived - jnp.dot(member, own_rows, precision=highest)
    residual_sums = jnp.dot(member.T, residual, precision=highest)
    counts = jnp.sum(member, axis=0)
    updated = own_rows + residual_sums / jnp.maximum(counts, 1.0)[:, None]
    residual_norm = jnp.sqrt(jnp.mean(residual * residual, axis=1) + epsilon)
    bin_hits = (bin_ids[:, None] == jnp.arange(NBINS, dtype=jnp.int32)[None, :]).astype(jnp.float32)
    histogram = jnp.dot(member.T, bin_hits * residual_norm[:, None], precision=highest)
    return (quant_error, updated, histogram)


def per_device(embeddings, centroids, assign, bins):
    owner_count = lax.axis_size("dp") * lax.axis_size("cent")
    if (2 * embeddings.shape[0] // owner_count) % 16 == 0:
        return per_device_kernel(embeddings, centroids, assign, bins)
    return per_device_plain(embeddings, centroids, assign, bins)


def solution(mesh):
    in_specs = (P(("dp", "cent"), None), P("cent", None), P(("dp", "cent")), P(("dp", "cent")))
    out_specs = (P(("dp", "cent")), P(("cent", "dp"), None), P(("cent", "dp"), None))
    return jax.shard_map(
        per_device, mesh=mesh, in_specs=in_specs, out_specs=out_specs, check_vma=False
    )
```

```python
import functools

import jax
import jax.numpy as jnp
from jax import lax
from jax.experimental import pallas as pl
from jax.experimental.pallas import tpu as pltpu
from jax.sharding import PartitionSpec as P

LISTS_DEV = 64
NBINS = 256

epsilon = 1e-06
MESH = pl.DeviceIdType.MESH
NT = (((1,), (1,)), ((), ()))


def kernel(
    n_dp, n_cent, cap,
    emb_hbm, cent_hbm, assign_hbm, bins_hbm,
    quant_ref, new_ref, hist_ref,
    assign_ref, bins_ref, emb_ref, outbuf, inbuf, mate_rows, pieces, min_out, min_in, code_out, code_z, codes,
    in_sem, own_sem,
    row_send, row_recv, mate_send, mate_recv, z_send, z_recv, p_send, p_recv, m_send, m_recv,
    cz_send, cz_recv, cp_send, cp_recv,
):
    rows, dim = emb_ref.shape
    chips, lists = pieces.shape[1], pieces.shape[2]
    owners = n_dp * n_cent
    slots = owners * cap
    width = n_dp * cap
    dp, ce = lax.axis_index("dp"), lax.axis_index("cent")
    chip, core = dp // 2, dp % 2
    mate = chip * 2 + (1 - core)
    me = ce * n_dp + dp

    loads = [
        pltpu.make_async_copy(a, b, in_sem.at[n])
        for n, (a, b) in enumerate(((assign_hbm, assign_ref), (bins_hbm, bins_ref), (emb_hbm, emb_ref)))
    ]
    for load in loads:
        load.start()

    def share(j):
        at = pl.multiple_of((j * 2 + core) * lists, lists)
        return pltpu.make_async_copy(cent_hbm.at[pl.ds(at, lists)], pieces.at[ce, j], own_sem.at[j])

    for j in range(chips):
        share(j).start()

    barrier = pltpu.get_barrier_semaphore()

    def greet(i, _):
        other = lax.rem(me + i, owners)
        pl.semaphore_signal(barrier, inc=1, device_id=(other % n_dp, other // n_dp), device_id_type=MESH)
        return 0

    lax.fori_loop(1, owners, greet, 0)
    for load in loads:
        load.wait()
    for j in range(chips):
        share(j).wait()

    shift = lists.bit_length() - 1
    assign = assign_ref[...]
    owner = lax.shift_right_logical(assign, shift)
    local = assign - lax.shift_left(owner, shift)
    hits = lax.broadcasted_iota(jnp.int32, (owners, rows), 0) == owner
    hits_f = hits.astype(jnp.float32)
    before = lax.broadcasted_iota(jnp.int32, (rows, rows), 0) < lax.broadcasted_iota(jnp.int32, (rows, rows), 1)
    earlier = jnp.dot(
        hits_f.astype(jnp.bfloat16),
        before.astype(jnp.float32).astype(jnp.bfloat16),
        preferred_element_type=jnp.float32,
    )
    place = jnp.sum(earlier * hits_f, axis=0, keepdims=True)
    position = owner * cap + place.astype(jnp.int32)
    pick = (lax.broadcasted_iota(jnp.int32, (slots, rows), 0) == position).astype(jnp.float32).astype(jnp.bfloat16)
    tag_row = lax.broadcasted_iota(jnp.int32, (16, rows), 0)
    tags = jnp.where(
        tag_row == 0,
        jnp.broadcast_to(local + 1, (16, rows)),
        jnp.where(tag_row == 1, jnp.broadcast_to(bins_ref[...], (16, rows)), 0),
    ).astype(jnp.float32).astype(jnp.bfloat16)
    outbuf[...] = (
        jnp.dot(pick, emb_ref[...], preferred_element_type=jnp.float32)
        .astype(jnp.bfloat16).reshape(owners, cap, dim)
    )
    slot_tags = lax.dot_general(tags, pick, NT, preferred_element_type=jnp.float32).astype(jnp.int32)
    code = slot_tags[0:1] * NBINS + slot_tags[1:2]
    for c in range(n_cent):
        code_out[c] = code[:, c * width:(c + 1) * width]

    pl.semaphore_wait(barrier, owners - 1)

    def z_copy(i):
        other = lax.rem(ce + i, n_cent)
        return pltpu.make_async_remote_copy(
            src_ref=pieces.at[ce, chip], dst_ref=pieces.at[ce, chip],
            send_sem=z_send.at[other], recv_sem=z_recv.at[ce],
            device_id=(dp, other), device_id_type=MESH,
        )

    def code_copy(i):
        other = lax.rem(ce + i, n_cent)
        return pltpu.make_async_remote_copy(
            src_ref=code_out.at[other], dst_ref=code_z.at[ce],
            send_sem=cz_send.at[other], recv_sem=cz_recv.at[ce],
            device_id=(dp, other), device_id_type=MESH,
        )

    def row_copy(other):
        return pltpu.make_async_remote_copy(
            src_ref=outbuf.at[other], dst_ref=inbuf.at[me],
            send_sem=row_send.at[other], recv_sem=row_recv.at[me],
            device_id=(other % n_dp, other // n_dp), device_id_type=MESH,
        )

    order = list(range(1, n_cent))
    for i in order:
        z_copy(i).start()
    for i in order:
        code_copy(i).start()
    mate_copy = pltpu.make_async_remote_copy(
        src_ref=emb_ref, dst_ref=mate_rows, send_sem=mate_send, recv_sem=mate_recv,
        device_id=(mate, ce), device_id_type=MESH,
    )
    mate_copy.start()

    def send_plane(i, _):
        row_copy(ce * n_dp + lax.rem(dp + i, n_dp)).start()
        return 0

    lax.fori_loop(1, n_dp, send_plane, 0)
    inbuf[me] = outbuf[me]
    code_z[ce] = code_out[ce]

    def plane_copy(i, block):
        other = lax.rem(chip + i, chips)
        return pltpu.make_async_remote_copy(
            src_ref=pieces.at[block, chip], dst_ref=pieces.at[block, chip],
            send_sem=p_send.at[block, other], recv_sem=p_recv.at[block, chip],
            device_id=(other * 2 + core, ce), device_id_type=MESH,
        )

    def arrive(ref, sem):
        return pltpu.make_async_copy(ref, ref, sem)

    def send_rows(i, _):
        gap = i // n_dp + 1
        other = lax.rem(ce + gap, n_cent) * n_dp + lax.rem(dp + i, n_dp)
        row_copy(other).start()
        return 0

    for gap in order:
        block = lax.rem(ce + gap, n_cent)
        arrive(pieces.at[block, chip], z_recv.at[block]).wait()
        for i in range(1, chips):
            plane_copy(i, block).start()
        lax.fori_loop((gap - 1) * n_dp, gap * n_dp, send_rows, 0)


    def spread_copy(i):
        other = lax.rem(dp + i, n_dp)
        return pltpu.make_async_remote_copy(
            src_ref=code_z, dst_ref=codes.at[dp],
            send_sem=cp_send.at[other], recv_sem=cp_recv.at[dp],
            device_id=(other, ce), device_id_type=MESH,
        )

    for gap in order:
        block = lax.rem(ce + gap, n_cent)
        arrive(code_z.at[block], cz_recv.at[block]).wait()
    for i in range(1, n_dp):
        spread_copy(i).start()
    codes[dp] = code_z[...]

    mate_copy.wait_recv()

    def nearest(block):
        piece = pieces[block].reshape(chips * lists, dim)
        piece_f = piece.astype(jnp.float32)
        sq = jnp.sum(piece_f * piece_f, axis=1, keepdims=True)
        own = lax.dot_general(piece, emb_ref[...], NT, preferred_element_type=jnp.float32)
        theirs = lax.dot_general(piece, mate_rows[...], NT, preferred_element_type=jnp.float32)
        return (
            jnp.min(sq - 2.0 * own, axis=0, keepdims=True),
            jnp.min(sq - 2.0 * theirs, axis=0, keepdims=True),
        )

    best = nearest(ce)
    emb_f = emb_ref[...].astype(jnp.float32)
    row_sq = jnp.sum(emb_f * emb_f, axis=1, keepdims=True)
    row_sq = jnp.broadcast_to(row_sq, (rows, 128)).T[0:1]

    def one_block(gap, best):
        block = lax.rem(ce + gap, n_cent)
        for i in range(1, chips):
            j = lax.rem(chip + i, chips)
            arrive(pieces.at[block, j], p_recv.at[block, j]).wait()
        found = nearest(block)
        return jnp.minimum(best[0], found[0]), jnp.minimum(best[1], found[1])

    best = lax.fori_loop(1, n_cent, one_block, best)

    min_out[...] = jnp.broadcast_to(best[1], min_out.shape)
    min_copy = pltpu.make_async_remote_copy(
        src_ref=min_out, dst_ref=min_in, send_sem=m_send, recv_sem=m_recv,
        device_id=(mate, ce), device_id_type=MESH,
    )
    min_copy.start()

    for i in range(1, n_dp):
        other = lax.rem(dp + i, n_dp)
        arrive(codes.at[other], cp_recv.at[other]).wait()
    every = jnp.concatenate([codes[d, c] for c in range(n_cent) for d in range(n_dp)], axis=0)
    list_tag = lax.shift_right_logical(every, 8)
    bin_tag = every - lax.shift_left(list_tag, 8)
    slot = lax.broadcasted_iota(jnp.int32, (slots, owners), 0)
    source = lax.broadcasted_iota(jnp.int32, (slots, owners), 1)
    low = slot - source * cap
    of_source = ((low >= 0) & (low < cap)).astype(jnp.float32).astype(jnp.bfloat16)
    lane = lax.broadcasted_iota(jnp.int32, (slots, width), 1)
    row_id = lax.broadcasted_iota(jnp.int32, (slots, width), 0)
    mine = lane == dp * cap + lax.rem(row_id, cap)

    def column(tag):
        spread = jnp.dot(
            of_source, tag.astype(jnp.float32).astype(jnp.bfloat16), preferred_element_type=jnp.float32
        )
        return jnp.sum(jnp.where(mine, spread, 0.0), axis=1, keepdims=True).astype(jnp.int32)

    list_col = column(list_tag) - 1
    bin_col = column(bin_tag)
    member = (lax.broadcasted_iota(jnp.int32, (slots, 128), 1) == list_col).astype(jnp.float32)
    member_t = member.T[:lists]
    member_b = member[:, :lists].astype(jnp.bfloat16)
    member_tb = member_t.astype(jnp.bfloat16)
    counts = jnp.sum(member_t, axis=1, keepdims=True)
    in_bin = lax.broadcasted_iota(jnp.int32, (slots, NBINS), 1) == bin_col
    own_rows = pieces[ce, chip]
    own_f = own_rows.astype(jnp.float32)
    own_spread = jnp.dot(member_b, own_rows, preferred_element_type=jnp.float32)

    min_copy.wait()
    quant_ref[...] = (jnp.minimum(best[0], min_in[0:1]) + row_sq) * (1.0 / dim)

    def wait_rows(i, _):
        other = lax.rem(me + i, owners)
        arrive(inbuf.at[other], row_recv.at[other]).wait()
        return 0

    lax.fori_loop(1, owners, wait_rows, 0)
    arrived = inbuf[...].reshape(slots, dim)
    sums = jnp.dot(member_tb, arrived, preferred_element_type=jnp.float32)
    new_ref[...] = own_f + (sums - counts * own_f) / jnp.maximum(counts, 1.0)
    residual = arrived.astype(jnp.float32) - own_spread
    norm = jnp.sqrt(jnp.sum(residual * residual, axis=1, keepdims=True) * (1.0 / dim) + epsilon)
    spread = jnp.where(in_bin, norm, 0.0)
    hist = jnp.zeros(hist_ref.shape, jnp.float32)
    for _ in range(3):
        part = spread.astype(jnp.bfloat16)
        hist = hist + jnp.dot(member_tb, part, preferred_element_type=jnp.float32)
        spread = spread - part.astype(jnp.float32)
    hist_ref[...] = hist

    mate_copy.wait_send()
    for i in order:
        z_copy(i).wait_send()
        code_copy(i).wait_send()
        for k in range(1, chips):
            plane_copy(k, lax.rem(ce + i, n_cent)).wait_send()
    for i in range(1, n_dp):
        spread_copy(i).wait_send()

    def sent(i, _):
        row_copy(lax.rem(me + i, owners)).wait_send()
        return 0

    lax.fori_loop(1, owners, sent, 0)


def per_device_kernel(embeddings, centroids, assign, bins):
    rows, dim = embeddings.shape
    n_dp, n_cent = lax.axis_size("dp"), lax.axis_size("cent")
    owners, chips = n_dp * n_cent, n_dp // 2
    cap = 2 * rows // owners
    lists = centroids.shape[0] // n_dp
    dma = pltpu.SemaphoreType.DMA
    vmem = pl.BlockSpec(memory_space=pltpu.VMEM)
    quant, new, hist = pl.pallas_call(
        functools.partial(kernel, n_dp, n_cent, cap),
        out_shape=(
            jax.ShapeDtypeStruct((1, rows), jnp.float32),
            jax.ShapeDtypeStruct((lists, dim), jnp.float32),
            jax.ShapeDtypeStruct((lists, NBINS), jnp.float32),
        ),
        in_specs=[pl.BlockSpec(memory_space=pltpu.HBM)] * 4,
        out_specs=(vmem,) * 3,
        scratch_shapes=[
            pltpu.VMEM((1, rows), jnp.int32),
            pltpu.VMEM((1, rows), jnp.int32),
            pltpu.VMEM((rows, dim), jnp.bfloat16),
            pltpu.VMEM((owners, cap, dim), jnp.bfloat16),
            pltpu.VMEM((owners, cap, dim), jnp.bfloat16),
            pltpu.VMEM((rows, dim), jnp.bfloat16),
            pltpu.VMEM((n_cent, chips, lists, dim), jnp.bfloat16),
            pltpu.VMEM((8, rows), jnp.float32),
            pltpu.VMEM((8, rows), jnp.float32),
            pltpu.VMEM((n_cent, 1, n_dp * cap), jnp.int32),
            pltpu.VMEM((n_cent, 1, n_dp * cap), jnp.int32),
            pltpu.VMEM((n_dp, n_cent, 1, n_dp * cap), jnp.int32),
            dma((3,)), dma((chips,)),
            dma((owners,)), dma((owners,)),
            dma, dma,
            dma((n_cent,)), dma((n_cent,)),
            dma((n_cent, chips)), dma((n_cent, chips)),
            dma, dma,
            dma((n_cent,)), dma((n_cent,)),
            dma((n_dp,)), dma((n_dp,)),
        ],
        compiler_params=pltpu.CompilerParams(
            collective_id=0, has_side_effects=True, vmem_limit_bytes=60 * 1024 * 1024
        ),
        cost_estimate=pl.CostEstimate(
            flops=2 * rows * 2048 * dim, bytes_accessed=4 * rows * dim * 2, transcendentals=0
        ),
    )(embeddings, centroids, assign.reshape(1, rows), bins.reshape(1, rows))
    return quant.reshape(rows), new, hist


def per_device_plain(embeddings, centroids, assign, bins):
    row_count, feature_dim = embeddings.shape
    row_f32 = embeddings.astype(jnp.float32)
    row_sq = jnp.sum(row_f32 * row_f32, axis=1)
    block_rows = lax.all_gather(centroids, "cent", axis=0, tiled=True)
    products = jnp.einsum("rd,kd->rk", embeddings, block_rows, preferred_element_type=jnp.float32)
    block_f32 = block_rows.astype(jnp.float32)
    cent_sq = jnp.sum(block_f32 * block_f32, axis=1)
    nearest_sq = jnp.min(cent_sq[None, :] - 2.0 * products, axis=1)
    quant_error = (nearest_sq + row_sq) / feature_dim
    dp_count = lax.axis_size("dp")
    cent_count = lax.axis_size("cent")
    owner_count = dp_count * cent_count
    slot_cap = 2 * row_count // owner_count
    owner_id = assign // LISTS_DEV
    local_list = assign % LISTS_DEV
    dest_slot = owner_id % dp_count * cent_count + owner_id // dp_count
    owner_hits = (dest_slot[:, None] == jnp.arange(owner_count, dtype=jnp.int32)[None, :]).astype(jnp.float32)
    row_ids = jnp.arange(row_count, dtype=jnp.int32)
    before = (row_ids[None, :] < row_ids[:, None]).astype(jnp.float32)
    earlier = jnp.dot(before, owner_hits)
    slot_id = jnp.sum(earlier * owner_hits, axis=1).astype(jnp.int32)
    position = dest_slot * slot_cap + slot_id
    outgoing = jnp.zeros((owner_count * slot_cap, feature_dim), jnp.bfloat16).at[position].set(embeddings)
    outgoing = outgoing.reshape(dp_count, cent_count, slot_cap, feature_dim)
    tag_values = jnp.stack([local_list, bins], axis=1).astype(jnp.float32)
    labels = jnp.full((owner_count * slot_cap, 2), -1.0, jnp.float32).at[position].set(tag_values)
    labels = labels.astype(jnp.bfloat16).reshape(dp_count, cent_count, slot_cap, 2)

    def exchange(x):
        x = lax.all_to_all(x, "dp", split_axis=0, concat_axis=0, tiled=True)
        return lax.all_to_all(x, "cent", split_axis=1, concat_axis=1, tiled=True)

    arrived = exchange(outgoing).reshape(-1, feature_dim).astype(jnp.float32)
    arrived_tags = exchange(labels).reshape(-1, 2).astype(jnp.int32)
    list_ids, bin_ids = arrived_tags[:, 0], arrived_tags[:, 1]
    member = (list_ids[:, None] == jnp.arange(LISTS_DEV, dtype=jnp.int32)[None, :]).astype(jnp.float32)
    own_rows = lax.dynamic_slice_in_dim(
        centroids, lax.axis_index("dp") * LISTS_DEV, LISTS_DEV, 0
    ).astype(jnp.float32)
    highest = lax.Precision.HIGHEST
    residual = arrived - jnp.dot(member, own_rows, precision=highest)
    residual_sums = jnp.dot(member.T, residual, precision=highest)
    counts = jnp.sum(member, axis=0)
    updated = own_rows + residual_sums / jnp.maximum(counts, 1.0)[:, None]
    residual_norm = jnp.sqrt(jnp.mean(residual * residual, axis=1) + epsilon)
    bin_hits = (bin_ids[:, None] == jnp.arange(NBINS, dtype=jnp.int32)[None, :]).astype(jnp.float32)
    histogram = jnp.dot(member.T, bin_hits * residual_norm[:, None], precision=highest)
    return (quant_error, updated, histogram)


def per_device(embeddings, centroids, assign, bins):
    n_dp = lax.axis_size("dp")
    cap = 2 * embeddings.shape[0] // (n_dp * lax.axis_size("cent"))
    if cap % 16 == 0 and n_dp * cap % 128 == 0:
        return per_device_kernel(embeddings, centroids, assign, bins)
    return per_device_plain(embeddings, centroids, assign, bins)


def solution(mesh):
    in_specs = (P(("dp", "cent"), None), P("cent", None), P(("dp", "cent")), P(("dp", "cent")))
    out_specs = (P(("dp", "cent")), P(("cent", "dp"), None), P(("cent", "dp"), None))
    return jax.shard_map(
        per_device, mesh=mesh, in_specs=in_specs, out_specs=out_specs, check_vma=False
    )
```

```python
import functools

import jax
import jax.numpy as jnp
from jax import lax
from jax.experimental import pallas as pl
from jax.experimental.pallas import tpu as pltpu
from jax.sharding import PartitionSpec as P

LISTS_DEV = 64
NBINS = 256

epsilon = 1e-06
MESH = pl.DeviceIdType.MESH
NT = (((1,), (1,)), ((), ()))


def kernel(
    n_dp, n_cent, cap,
    emb_hbm, cent_hbm, assign_hbm, bins_hbm,
    quant_ref, new_ref, hist_ref,
    assign_ref, bins_ref, group, outbuf, inbuf, pieces, min_out, min_in, code_out, code_z, codes,
    in_sem, own_sem,
    row_send, row_recv, g_send, g_recv, up_send, down_send, z_recv, y_send, y_recv, m_send, m_recv,
    cz_send, cz_recv, cp_send, cp_recv,
):
    rows, dim = group.shape[1:]
    span, lists = pieces.shape[1], pieces.shape[2]
    owners = n_dp * n_cent
    slots = owners * cap
    width = n_dp * cap
    dp, ce = lax.axis_index("dp"), lax.axis_index("cent")
    y, x, core = dp // 4, (dp // 2) % 2, dp % 2
    mate = y * 4 + x * 2 + (1 - core)
    beside = y * 4 + (1 - x) * 2 + core
    across = y * 4 + (1 - x) * 2 + (1 - core)
    emb_ref = group.at[3]
    me = ce * n_dp + dp

    loads = [
        pltpu.make_async_copy(a, b, in_sem.at[n])
        for n, (a, b) in enumerate(((assign_hbm, assign_ref), (bins_hbm, bins_ref), (emb_hbm, emb_ref)))
    ]
    for load in loads:
        load.start()

    def share(j):
        at = pl.multiple_of(((j * 2 + x) * 2 + core) * lists, lists)
        return pltpu.make_async_copy(cent_hbm.at[pl.ds(at, lists)], pieces.at[ce, j], own_sem.at[j])

    for j in range(span):
        share(j).start()

    barrier = pltpu.get_barrier_semaphore()

    def greet(i, _):
        other = lax.rem(me + i, owners)
        pl.semaphore_signal(barrier, inc=1, device_id=(other % n_dp, other // n_dp), device_id_type=MESH)
        return 0

    lax.fori_loop(1, owners, greet, 0)
    for load in loads:
        load.wait()
    for j in range(span):
        share(j).wait()

    shift = lists.bit_length() - 1
    assign = assign_ref[...]
    owner = lax.shift_right_logical(assign, shift)
    local = assign - lax.shift_left(owner, shift)
    hits = lax.broadcasted_iota(jnp.int32, (owners, rows), 0) == owner
    hits_f = hits.astype(jnp.float32)
    before = lax.broadcasted_iota(jnp.int32, (rows, rows), 0) < lax.broadcasted_iota(jnp.int32, (rows, rows), 1)
    earlier = jnp.dot(
        hits_f.astype(jnp.bfloat16),
        before.astype(jnp.float32).astype(jnp.bfloat16),
        preferred_element_type=jnp.float32,
    )
    place = jnp.sum(earlier * hits_f, axis=0, keepdims=True)
    position = owner * cap + place.astype(jnp.int32)
    pick = (lax.broadcasted_iota(jnp.int32, (slots, rows), 0) == position).astype(jnp.float32).astype(jnp.bfloat16)
    tag_row = lax.broadcasted_iota(jnp.int32, (16, rows), 0)
    tags = jnp.where(
        tag_row == 0,
        jnp.broadcast_to(local + 1, (16, rows)),
        jnp.where(tag_row == 1, jnp.broadcast_to(bins_ref[...], (16, rows)), 0),
    ).astype(jnp.float32).astype(jnp.bfloat16)
    outbuf[...] = (
        jnp.dot(pick, emb_ref[...], preferred_element_type=jnp.float32)
        .astype(jnp.bfloat16).reshape(owners, cap, dim)
    )
    slot_tags = lax.dot_general(tags, pick, NT, preferred_element_type=jnp.float32).astype(jnp.int32)
    code = slot_tags[0:1] * NBINS + slot_tags[1:2]
    for c in range(n_cent):
        code_out[c] = code[:, c * width:(c + 1) * width]

    pl.semaphore_wait(barrier, owners - 1)

    def z_copy(block, step, sems):
        return pltpu.make_async_remote_copy(
            src_ref=pieces.at[block, y], dst_ref=pieces.at[block, y],
            send_sem=sems.at[block], recv_sem=z_recv.at[block],
            device_id=(dp, ce + step), device_id_type=MESH,
        )

    def code_copy(i):
        other = lax.rem(ce + i, n_cent)
        return pltpu.make_async_remote_copy(
            src_ref=code_out.at[other], dst_ref=code_z.at[ce],
            send_sem=cz_send.at[other], recv_sem=cz_recv.at[ce],
            device_id=(dp, other), device_id_type=MESH,
        )

    def row_copy(other):
        return pltpu.make_async_remote_copy(
            src_ref=outbuf.at[other], dst_ref=inbuf.at[me],
            send_sem=row_send.at[other], recv_sem=row_recv.at[me],
            device_id=(other % n_dp, other // n_dp), device_id_type=MESH,
        )

    order = list(range(1, n_cent))

    @pl.when(ce + 1 < n_cent)
    def _():
        z_copy(ce, 1, up_send).start()

    @pl.when(ce > 0)
    def _():
        z_copy(ce, -1, down_send).start()

    for i in order:
        code_copy(i).start()

    def group_copy(source, slot, other):
        return pltpu.make_async_remote_copy(
            src_ref=group.at[source], dst_ref=group.at[slot],
            send_sem=g_send.at[slot], recv_sem=g_recv.at[slot],
            device_id=(other, ce), device_id_type=MESH,
        )

    group_copy(3, 1, beside).start()
    group_copy(3, 0, mate).start()

    def send_plane(i, _):
        row_copy(ce * n_dp + lax.rem(dp + i, n_dp)).start()
        return 0

    lax.fori_loop(1, n_dp, send_plane, 0)
    inbuf[me] = outbuf[me]
    code_z[ce] = code_out[ce]

    def y_copy(i, block):
        other = lax.rem(y + i, span)
        return pltpu.make_async_remote_copy(
            src_ref=pieces.at[block, y], dst_ref=pieces.at[block, y],
            send_sem=y_send.at[block, other], recv_sem=y_recv.at[block, y],
            device_id=(other * 4 + x * 2 + core, ce), device_id_type=MESH,
        )

    def arrive(ref, sem):
        return pltpu.make_async_copy(ref, ref, sem)

    def send_rows(i, _):
        gap = i // n_dp + 1
        other = lax.rem(ce + gap, n_cent) * n_dp + lax.rem(dp + i, n_dp)
        row_copy(other).start()
        return 0

    for gap in order:

        @pl.when(ce >= gap)
        def _():
            block = ce - gap
            arrive(pieces.at[block, y], z_recv.at[block]).wait()

            @pl.when(ce + 1 < n_cent)
            def _():
                z_copy(block, 1, up_send).start()

            for i in range(1, span):
                y_copy(i, block).start()

        @pl.when(ce + gap < n_cent)
        def _():
            block = ce + gap
            arrive(pieces.at[block, y], z_recv.at[block]).wait()

            @pl.when(ce > 0)
            def _():
                z_copy(block, -1, down_send).start()

            for i in range(1, span):
                y_copy(i, block).start()


    lax.fori_loop(0, owners - n_dp, send_rows, 0)

    def spread_copy(i):
        other = lax.rem(dp + i, n_dp)
        return pltpu.make_async_remote_copy(
            src_ref=code_z, dst_ref=codes.at[dp],
            send_sem=cp_send.at[other], recv_sem=cp_recv.at[dp],
            device_id=(other, ce), device_id_type=MESH,
        )

    for gap in order:
        block = lax.rem(ce + gap, n_cent)
        arrive(code_z.at[block], cz_recv.at[block]).wait()
    for i in range(1, n_dp):
        spread_copy(i).start()
    codes[dp] = code_z[...]

    arrive(group.at[1], g_recv.at[1]).wait()
    group_copy(1, 2, mate).start()
    arrive(group.at[0], g_recv.at[0]).wait()
    arrive(group.at[2], g_recv.at[2]).wait()

    def nearest(block):
        piece = pieces[block].reshape(span * lists, dim)
        piece_f = piece.astype(jnp.float32)
        sq = jnp.sum(piece_f * piece_f, axis=1, keepdims=True)
        products = lax.dot_general(piece, group[...].reshape(4 * rows, dim), NT, preferred_element_type=jnp.float32)
        return jnp.min(sq - 2.0 * products, axis=0, keepdims=True)

    best = nearest(ce)
    emb_f = emb_ref[...].astype(jnp.float32)
    row_sq = jnp.sum(emb_f * emb_f, axis=1, keepdims=True)
    row_sq = jnp.broadcast_to(row_sq, (rows, 128)).T[0:1]

    def one_block(gap, best):
        block = lax.rem(ce + gap, n_cent)
        for i in range(1, span):
            j = lax.rem(y + i, span)
            arrive(pieces.at[block, j], y_recv.at[block, j]).wait()
        return jnp.minimum(best, nearest(block))

    best = lax.fori_loop(1, n_cent, one_block, best)

    def min_copy(n):
        return pltpu.make_async_remote_copy(
            src_ref=min_out.at[n], dst_ref=min_in.at[n], send_sem=m_send.at[n], recv_sem=m_recv.at[n],
            device_id=((mate, beside, across)[n], ce), device_id_type=MESH,
        )

    for n in range(3):
        min_out[n] = jnp.broadcast_to(best[:, n * rows:(n + 1) * rows], min_out.shape[1:])
        min_copy(n).start()

    for i in range(1, n_dp):
        other = lax.rem(dp + i, n_dp)
        arrive(codes.at[other], cp_recv.at[other]).wait()
    every = jnp.concatenate([codes[d, c] for c in range(n_cent) for d in range(n_dp)], axis=0)
    list_tag = lax.shift_right_logical(every, 8)
    bin_tag = every - lax.shift_left(list_tag, 8)
    slot = lax.broadcasted_iota(jnp.int32, (slots, owners), 0)
    source = lax.broadcasted_iota(jnp.int32, (slots, owners), 1)
    low = slot - source * cap
    of_source = ((low >= 0) & (low < cap)).astype(jnp.float32).astype(jnp.bfloat16)
    lane = lax.broadcasted_iota(jnp.int32, (slots, width), 1)
    row_id = lax.broadcasted_iota(jnp.int32, (slots, width), 0)
    mine = lane == dp * cap + lax.rem(row_id, cap)

    def column(tag):
        spread = jnp.dot(
            of_source, tag.astype(jnp.float32).astype(jnp.bfloat16), preferred_element_type=jnp.float32
        )
        return jnp.sum(jnp.where(mine, spread, 0.0), axis=1, keepdims=True).astype(jnp.int32)

    list_col = column(list_tag) - 1
    bin_col = column(bin_tag)
    member = (lax.broadcasted_iota(jnp.int32, (slots, 128), 1) == list_col).astype(jnp.float32)
    member_t = member.T[:lists]
    member_b = member[:, :lists].astype(jnp.bfloat16)
    member_tb = member_t.astype(jnp.bfloat16)
    counts = jnp.sum(member_t, axis=1, keepdims=True)
    in_bin = lax.broadcasted_iota(jnp.int32, (slots, NBINS), 1) == bin_col
    own_rows = pieces[ce, y]
    own_f = own_rows.astype(jnp.float32)
    own_spread = jnp.dot(member_b, own_rows, preferred_element_type=jnp.float32)

    least = best[:, 3 * rows:]
    for n in range(3):
        min_copy(n).wait()
        least = jnp.minimum(least, min_in[n, 0:1])
    quant_ref[...] = (least + row_sq) * (1.0 / dim)

    def wait_rows(i, _):
        other = lax.rem(me + i, owners)
        arrive(inbuf.at[other], row_recv.at[other]).wait()
        return 0

    lax.fori_loop(1, owners, wait_rows, 0)
    arrived = inbuf[...].reshape(slots, dim)
    sums = jnp.dot(member_tb, arrived, preferred_element_type=jnp.float32)
    new_ref[...] = own_f + (sums - counts * own_f) / jnp.maximum(counts, 1.0)
    residual = arrived.astype(jnp.float32) - own_spread
    norm = jnp.sqrt(jnp.sum(residual * residual, axis=1, keepdims=True) * (1.0 / dim) + epsilon)
    spread = jnp.where(in_bin, norm, 0.0)
    hist = jnp.zeros(hist_ref.shape, jnp.float32)
    for _ in range(3):
        part = spread.astype(jnp.bfloat16)
        hist = hist + jnp.dot(member_tb, part, preferred_element_type=jnp.float32)
        spread = spread - part.astype(jnp.float32)
    hist_ref[...] = hist

    group_copy(3, 1, beside).wait_send()
    group_copy(3, 0, mate).wait_send()
    group_copy(1, 2, mate).wait_send()

    @pl.when(ce + 1 < n_cent)
    def _():
        lax.fori_loop(0, ce + 1, lambda b, _: (z_copy(b, 1, up_send).wait_send(), 0)[1], 0)

    @pl.when(ce > 0)
    def _():
        lax.fori_loop(ce, n_cent, lambda b, _: (z_copy(b, -1, down_send).wait_send(), 0)[1], 0)

    for i in order:
        code_copy(i).wait_send()
        for k in range(1, span):
            y_copy(k, lax.rem(ce + i, n_cent)).wait_send()
    for i in range(1, n_dp):
        spread_copy(i).wait_send()

    def sent(i, _):
        row_copy(lax.rem(me + i, owners)).wait_send()
        return 0

    lax.fori_loop(1, owners, sent, 0)


def per_device_kernel(embeddings, centroids, assign, bins):
    rows, dim = embeddings.shape
    n_dp, n_cent = lax.axis_size("dp"), lax.axis_size("cent")
    owners, span = n_dp * n_cent, n_dp // 4
    cap = 2 * rows // owners
    lists = centroids.shape[0] // n_dp
    dma = pltpu.SemaphoreType.DMA
    vmem = pl.BlockSpec(memory_space=pltpu.VMEM)
    quant, new, hist = pl.pallas_call(
        functools.partial(kernel, n_dp, n_cent, cap),
        out_shape=(
            jax.ShapeDtypeStruct((1, rows), jnp.float32),
            jax.ShapeDtypeStruct((lists, dim), jnp.float32),
            jax.ShapeDtypeStruct((lists, NBINS), jnp.float32),
        ),
        in_specs=[pl.BlockSpec(memory_space=pltpu.HBM)] * 4,
        out_specs=(vmem,) * 3,
        scratch_shapes=[
            pltpu.VMEM((1, rows), jnp.int32),
            pltpu.VMEM((1, rows), jnp.int32),
            pltpu.VMEM((4, rows, dim), jnp.bfloat16),
            pltpu.VMEM((owners, cap, dim), jnp.bfloat16),
            pltpu.VMEM((owners, cap, dim), jnp.bfloat16),
            pltpu.VMEM((n_cent, span, lists, dim), jnp.bfloat16),
            pltpu.VMEM((3, 8, rows), jnp.float32),
            pltpu.VMEM((3, 8, rows), jnp.float32),
            pltpu.VMEM((n_cent, 1, n_dp * cap), jnp.int32),
            pltpu.VMEM((n_cent, 1, n_dp * cap), jnp.int32),
            pltpu.VMEM((n_dp, n_cent, 1, n_dp * cap), jnp.int32),
            dma((3,)), dma((span,)),
            dma((owners,)), dma((owners,)),
            dma((3,)), dma((3,)),
            dma((n_cent,)), dma((n_cent,)), dma((n_cent,)),
            dma((n_cent, span)), dma((n_cent, span)),
            dma((3,)), dma((3,)),
            dma((n_cent,)), dma((n_cent,)),
            dma((n_dp,)), dma((n_dp,)),
        ],
        compiler_params=pltpu.CompilerParams(
            collective_id=0, has_side_effects=True, vmem_limit_bytes=60 * 1024 * 1024
        ),
        cost_estimate=pl.CostEstimate(
            flops=2 * rows * 2048 * dim, bytes_accessed=4 * rows * dim * 2, transcendentals=0
        ),
    )(embeddings, centroids, assign.reshape(1, rows), bins.reshape(1, rows))
    return quant.reshape(rows), new, hist


def per_device_plain(embeddings, centroids, assign, bins):
    row_count, feature_dim = embeddings.shape
    row_f32 = embeddings.astype(jnp.float32)
    row_sq = jnp.sum(row_f32 * row_f32, axis=1)
    block_rows = lax.all_gather(centroids, "cent", axis=0, tiled=True)
    products = jnp.einsum("rd,kd->rk", embeddings, block_rows, preferred_element_type=jnp.float32)
    block_f32 = block_rows.astype(jnp.float32)
    cent_sq = jnp.sum(block_f32 * block_f32, axis=1)
    nearest_sq = jnp.min(cent_sq[None, :] - 2.0 * products, axis=1)
    quant_error = (nearest_sq + row_sq) / feature_dim
    dp_count = lax.axis_size("dp")
    cent_count = lax.axis_size("cent")
    owner_count = dp_count * cent_count
    slot_cap = 2 * row_count // owner_count
    owner_id = assign // LISTS_DEV
    local_list = assign % LISTS_DEV
    dest_slot = owner_id % dp_count * cent_count + owner_id // dp_count
    owner_hits = (dest_slot[:, None] == jnp.arange(owner_count, dtype=jnp.int32)[None, :]).astype(jnp.float32)
    row_ids = jnp.arange(row_count, dtype=jnp.int32)
    before = (row_ids[None, :] < row_ids[:, None]).astype(jnp.float32)
    earlier = jnp.dot(before, owner_hits)
    slot_id = jnp.sum(earlier * owner_hits, axis=1).astype(jnp.int32)
    position = dest_slot * slot_cap + slot_id
    outgoing = jnp.zeros((owner_count * slot_cap, feature_dim), jnp.bfloat16).at[position].set(embeddings)
    outgoing = outgoing.reshape(dp_count, cent_count, slot_cap, feature_dim)
    tag_values = jnp.stack([local_list, bins], axis=1).astype(jnp.float32)
    labels = jnp.full((owner_count * slot_cap, 2), -1.0, jnp.float32).at[position].set(tag_values)
    labels = labels.astype(jnp.bfloat16).reshape(dp_count, cent_count, slot_cap, 2)

    def exchange(x):
        x = lax.all_to_all(x, "dp", split_axis=0, concat_axis=0, tiled=True)
        return lax.all_to_all(x, "cent", split_axis=1, concat_axis=1, tiled=True)

    arrived = exchange(outgoing).reshape(-1, feature_dim).astype(jnp.float32)
    arrived_tags = exchange(labels).reshape(-1, 2).astype(jnp.int32)
    list_ids, bin_ids = arrived_tags[:, 0], arrived_tags[:, 1]
    member = (list_ids[:, None] == jnp.arange(LISTS_DEV, dtype=jnp.int32)[None, :]).astype(jnp.float32)
    own_rows = lax.dynamic_slice_in_dim(
        centroids, lax.axis_index("dp") * LISTS_DEV, LISTS_DEV, 0
    ).astype(jnp.float32)
    highest = lax.Precision.HIGHEST
    residual = arrived - jnp.dot(member, own_rows, precision=highest)
    residual_sums = jnp.dot(member.T, residual, precision=highest)
    counts = jnp.sum(member, axis=0)
    updated = own_rows + residual_sums / jnp.maximum(counts, 1.0)[:, None]
    residual_norm = jnp.sqrt(jnp.mean(residual * residual, axis=1) + epsilon)
    bin_hits = (bin_ids[:, None] == jnp.arange(NBINS, dtype=jnp.int32)[None, :]).astype(jnp.float32)
    histogram = jnp.dot(member.T, bin_hits * residual_norm[:, None], precision=highest)
    return (quant_error, updated, histogram)


def per_device(embeddings, centroids, assign, bins):
    n_dp = lax.axis_size("dp")
    cap = 2 * embeddings.shape[0] // (n_dp * lax.axis_size("cent"))
    if cap % 16 == 0 and n_dp * cap % 128 == 0 and n_dp % 4 == 0:
        return per_device_kernel(embeddings, centroids, assign, bins)
    return per_device_plain(embeddings, centroids, assign, bins)


def solution(mesh):
    in_specs = (P(("dp", "cent"), None), P("cent", None), P(("dp", "cent")), P(("dp", "cent")))
    out_specs = (P(("dp", "cent")), P(("cent", "dp"), None), P(("cent", "dp"), None))
    return jax.shard_map(
        per_device, mesh=mesh, in_specs=in_specs, out_specs=out_specs, check_vma=False
    )
```
